32 devices in a mesh: ctx: 16 (over z, x, core), heads: 2 (over y).
Axes of the slice: x: 2, y: 2, z: 4, core: 2. Of those that a mesh axis runs over, the one named last changes fastest.
Arguments:
- hidden: bfloat16 [8192, 5376], P(('ctx', 'heads')), may hold values from -8 to 8
- query_weight: bfloat16 [5376, 2048], P(None, 'heads'), may hold values from -0.5 to 0.5
- key_weight: bfloat16 [5376, 1024], P(None, 'heads'), may hold values from -0.5 to 0.5
- value_weight: bfloat16 [5376, 1024], P(None, 'heads'), may hold values from -0.078125 to 0.078125
- query_gain: float32 [128], replicated, may hold values from 0.5 to 6
- key_gain: float32 [128], replicated, may hold values from 0.5 to 6
- out_grad: bfloat16 [8192, 2048], P('ctx', 'heads'), may hold values from -6 to 6
Outputs:
- attention: bfloat16 [8192, 2048], P('ctx', 'heads')
- input_grad: bfloat16 [8192, 5376], P(('ctx', 'heads'))
- query_weight_grad: float32 [5376, 2048], P('ctx', 'heads')
- key_weight_grad: float32 [5376, 1024], P('ctx', 'heads')
- value_weight_grad: float32 [5376, 1024], P('ctx', 'heads')
The draws below stay inside these ranges and needn't reach their ends.
All inputs are finite; a program needn't handle non-finite values.
Results may differ from the reference program's by a relative error of at most 0.039.
Values may be sent and summed in bfloat16 or wider, within the bound.
A program may use at most 192 MiB of HBM per device.

```python
import math
import jax
import jax.numpy as jnp
from jax import lax

D = 5376
HEAD_DIM = 128
WINDOW = 1024
SCALAR = 168
HEADS = 16
KV_HEADS = 8
TOK_DEV = 512
TOKENS = 8192
HEAD_GROUPS = 2


def key_columns(key):
    return jax.random.normal(jax.random.fold_in(key, 7), (D, KV_HEADS * HEAD_DIM), jnp.float32) * D ** (-0.5)


def draw_key_weight(key, part):
    return jnp.clip(key_columns(key), -0.5, 0.5).astype(jnp.bfloat16)


def draw_query_weight(key, part):
    independent = jax.random.normal(jax.random.fold_in(key, 11), (D, HEADS * HEAD_DIM), jnp.float32) * D ** (-0.5)
    return jnp.clip(independent, -0.5, 0.5).astype(jnp.bfloat16)


def draw_hidden(key, part):
    values = jax.random.normal(jax.random.fold_in(key, 29), (TOKENS, D), jnp.float32)
    return jnp.clip(values, -8.0, 8.0).astype(jnp.bfloat16)


def channel_gains(key, salt_value):
    return jax.random.uniform(jax.random.fold_in(key, salt_value), (HEAD_DIM,), jnp.float32, 0.5, 1.5)


def draw_query_gain(key, part):
    return channel_gains(key, 41)


def draw_key_gain(key, part):
    return channel_gains(key, 43)


def block_levels(stream_key, shape, cuts, low, high):
    def one(position, parts):
        draws = jax.random.uniform(jax.random.fold_in(jax.random.fold_in(stream_key, 6), position), (parts,), jnp.float32, low / len(cuts), high / len(cuts))
        return jnp.repeat(jnp.exp(draws), shape[position] // parts).reshape((-1,) + (1,) * (len(shape) - position - 1))

    loudness = one(*cuts[0])
    for cut in cuts[1:]:
        loudness = loudness * one(*cut)
    return loudness


def bell_draw(rng, extent, scale, bound, split=(), held_as=jnp.bfloat16):
    drawn = scale * jax.random.normal(rng, extent, jnp.float32)
    if split:
        drawn = drawn * block_levels(rng, extent, split, -0.22, 0.18)
    return jnp.clip(drawn, -bound, bound).astype(held_as)


def setup_inputs(seed: int = 0) -> dict:
    arg_keys = jax.random.split(jax.random.key(seed), 8)
    hidden = draw_hidden(jax.random.fold_in(arg_keys[7], 71), 0)
    query_weight = draw_query_weight(jax.random.fold_in(arg_keys[7], 71), 0)
    key_weight = draw_key_weight(jax.random.fold_in(arg_keys[7], 71), 0)
    value_weight = bell_draw(arg_keys[3], (D, KV_HEADS * HEAD_DIM), D ** -0.5, 0.078125, ((1, 2),))
    query_gain = draw_query_gain(jax.random.fold_in(arg_keys[7], 71), 0)
    key_gain = draw_key_gain(jax.random.fold_in(arg_keys[7], 71), 0)
    out_grad = bell_draw(arg_keys[6], (TOKENS, HEADS * HEAD_DIM), 1.0, 6.0, ((0, 16), (1, 2)))
    return {"hidden": hidden, "query_weight": query_weight, "key_weight": key_weight, "value_weight": value_weight, "query_gain": query_gain, "key_gain": key_gain, "out_grad": out_grad}


def rope_tables(positions, head_size):
    half_size = head_size // 2
    indices = jnp.arange(half_size, dtype=jnp.float32)
    inverse = jnp.exp(indices * (-2.0 * math.log(10000.0) / head_size))
    angles = positions.astype(jnp.float32)[:, None] * inverse[None, :]
    return (jnp.cos(angles), jnp.sin(angles))

def prepare(projected, cosine, sine_table, channel_gain, factor):
    row_count = projected.shape[0]
    head_size = channel_gain.shape[0]
    pieces = projected.reshape(row_count, -1, head_size)
    normed = pieces * lax.rsqrt(lax.optimization_barrier(jnp.mean(pieces * pieces, axis=-1, keepdims=True)) + 1e-06) * channel_gain
    half_size = head_size // 2
    leading = normed[..., :half_size]
    trailing = normed[..., half_size:]
    cos_rows = cosine[:, None, :]
    sin_rows = sine_table[:, None, :]
    turned = jnp.concatenate([leading * cos_rows - trailing * sin_rows, trailing * cos_rows + leading * sin_rows], axis=-1)
    return (turned * factor).reshape(row_count, -1)

def band_mask(query_pos, key_pos):
    separation = query_pos[:, None] - key_pos[None, :]
    return (separation >= 0) & (separation < WINDOW) & (key_pos[None, :] >= 0)

def head_grids(query_block, key_window, value_window, group_size):
    query_grid = query_block.reshape(query_block.shape[0], -1, group_size, HEAD_DIM).astype(jnp.float32)
    key_grid = key_window.reshape(key_window.shape[0], -1, HEAD_DIM).astype(jnp.float32)
    value_grid = value_window.reshape(value_window.shape[0], -1, HEAD_DIM).astype(jnp.float32)
    return (query_grid, key_grid, value_grid)

def attend_forward(query_block, key_window, value_window, allowed, group_size):
    query_grid, key_grid, value_grid = head_grids(query_block, key_window, value_window, group_size)
    scores = jnp.einsum('qkgd,jkd->kgqj', query_grid, key_grid)
    masked = jnp.where(allowed, scores, -1e+30)
    highest = lax.optimization_barrier(jnp.max(masked, axis=-1, keepdims=True))
    total = lax.optimization_barrier(jnp.sum(jnp.exp(masked - highest), axis=-1, keepdims=True))
    log_total = highest + jnp.log(total)
    weights = jnp.where(allowed, jnp.exp(masked - log_total), 0.0)
    weights_low = lax.optimization_barrier(weights.astype(jnp.bfloat16)).astype(jnp.float32)
    output = jnp.einsum('kgqj,jkd->qkgd', weights_low, value_grid)
    return (output.reshape(query_block.shape[0], -1), log_total[..., 0])

def attend_backward(query_block, key_window, value_window, allowed, log_total, out_block, attention_block, group_size):
    query_grid, key_grid, value_grid = head_grids(query_block, key_window, value_window, group_size)
    row_count = query_block.shape[0]
    grad_grid = out_block.reshape(row_count, -1, group_size, HEAD_DIM).astype(jnp.float32)
    attention_grid = attention_block.reshape(row_count, -1, group_size, HEAD_DIM).astype(jnp.float32)
    scores = jnp.einsum('qkgd,jkd->kgqj', query_grid, key_grid)
    masked = jnp.where(allowed, scores, -1e+30)
    weights = jnp.where(allowed, jnp.exp(masked - log_total[..., None]), 0.0)
    weights_low = lax.optimization_barrier(weights.astype(jnp.bfloat16)).astype(jnp.float32)
    delta = jnp.einsum('qkgd,qkgd->kgq', grad_grid, attention_grid)
    products = jnp.einsum('qkgd,jkd->kgqj', grad_grid, value_grid)
    shifts = (weights * (products - delta[..., None])).astype(jnp.bfloat16)
    shifts = lax.optimization_barrier(shifts).astype(jnp.float32)
    query_cot = jnp.einsum('kgqj,jkd->qkgd', shifts, key_grid).reshape(row_count, -1)
    key_cot = jnp.einsum('kgqj,qkgd->jkd', shifts, query_grid).reshape(key_window.shape[0], -1)
    value_cot = jnp.einsum('kgqj,qkgd->jkd', weights_low, grad_grid).reshape(key_window.shape[0], -1)
    return (query_cot, key_cot, value_cot)

def reference(hidden, query_weight, key_weight, value_weight, query_gain, key_gain, out_grad):
    group_size = HEADS // KV_HEADS
    block_rows = min(TOK_DEV, 512)
    block_count = TOKENS // block_rows
    window_rows = block_rows + WINDOW
    positions = jnp.arange(TOKENS, dtype=jnp.int32)
    cosine, sine_table = rope_tables(positions, HEAD_DIM)
    query_proj = jnp.dot(hidden, query_weight, preferred_element_type=jnp.float32)
    key_proj = jnp.dot(hidden, key_weight, preferred_element_type=jnp.float32)
    value_proj = jnp.dot(hidden, value_weight, preferred_element_type=jnp.float32)
    query_full, query_back = jax.vjp(lambda projected: prepare(projected, cosine, sine_table, query_gain, SCALAR ** (-0.5)), query_proj)
    key_full, key_back = jax.vjp(lambda projected: prepare(projected, cosine, sine_table, key_gain, 1.0), key_proj)
    query_cast = lax.optimization_barrier(query_full.astype(jnp.bfloat16))
    key_cast = lax.optimization_barrier(key_full.astype(jnp.bfloat16))
    value_cast = lax.optimization_barrier(value_proj.astype(jnp.bfloat16))
    key_padded = jnp.pad(key_cast, ((WINDOW, 0), (0, 0)))
    value_padded = jnp.pad(value_cast, ((WINDOW, 0), (0, 0)))

    def window_of(block_index):
        block_start = block_index * block_rows
        query_block = lax.dynamic_slice_in_dim(query_cast, block_start, block_rows, 0)
        key_window = lax.dynamic_slice_in_dim(key_padded, block_start, window_rows, 0)
        value_window = lax.dynamic_slice_in_dim(value_padded, block_start, window_rows, 0)
        query_pos = block_start + jnp.arange(block_rows, dtype=jnp.int32)
        key_pos = block_start - WINDOW + jnp.arange(window_rows, dtype=jnp.int32)
        return (query_block, key_window, value_window, band_mask(query_pos, key_pos))

    def forward_block(block_index):
        query_block, key_window, value_window, allowed = window_of(block_index)
        return attend_forward(query_block, key_window, value_window, allowed, group_size)
    outputs, log_totals = lax.map(forward_block, jnp.arange(block_count, dtype=jnp.int32))
    attention = outputs.reshape(TOKENS, -1).astype(jnp.bfloat16)

    def backward_block(carry, block_index):
        key_acc, value_acc = carry
        query_block, key_window, value_window, allowed = window_of(block_index)
        block_start = block_index * block_rows
        out_block = lax.dynamic_slice_in_dim(out_grad, block_start, block_rows, 0)
        attention_block = lax.dynamic_slice_in_dim(attention, block_start, block_rows, 0)
        query_cot, key_cot, value_cot = attend_backward(query_block, key_window, value_window, allowed, log_totals[block_index], out_block, attention_block, group_size)
        key_region = lax.dynamic_slice_in_dim(key_acc, block_start, window_rows, 0) + key_cot
        value_region = lax.dynamic_slice_in_dim(value_acc, block_start, window_rows, 0) + value_cot
        key_acc = lax.dynamic_update_slice_in_dim(key_acc, key_region, block_start, 0)
        value_acc = lax.dynamic_update_slice_in_dim(value_acc, value_region, block_start, 0)
        return ((key_acc, value_acc), query_cot)
    zero_rows = jnp.zeros((TOKENS + WINDOW, KV_HEADS * HEAD_DIM), jnp.float32)
    (key_acc, value_acc), query_cots = lax.scan(backward_block, (zero_rows, zero_rows), jnp.arange(block_count, dtype=jnp.int32))
    grad_query = query_back(query_cots.reshape(TOKENS, -1))[0].astype(jnp.bfloat16)
    grad_key = key_back(key_acc[WINDOW:])[0].astype(jnp.bfloat16)
    grad_value = value_acc[WINDOW:].astype(jnp.bfloat16)
    grad_scale = float(TOKENS) ** (-0.5)
    contract = (((0,), (0,)), ((), ()))
    query_weight_grad = lax.dot_general(hidden, grad_query, contract, preferred_element_type=jnp.float32) * grad_scale
    key_weight_grad = lax.dot_general(hidden, grad_key, contract, preferred_element_type=jnp.float32) * grad_scale
    value_weight_grad = lax.dot_general(hidden, grad_value, contract, preferred_element_type=jnp.float32) * grad_scale
    query_width = HEADS * HEAD_DIM // HEAD_GROUPS
    key_width = KV_HEADS * HEAD_DIM // HEAD_GROUPS
    back_contract = (((1,), (1,)), ((), ()))
    input_sum = jnp.zeros((TOKENS, D), jnp.float32)
    for group_index in range(HEAD_GROUPS):
        query_lower = group_index * query_width
        key_lower = group_index * key_width
        group_term = lax.dot_general(grad_query[:, query_lower:query_lower + query_width], query_weight[:, query_lower:query_lower + query_width], back_contract, preferred_element_type=jnp.float32)
        group_term = group_term + lax.dot_general(grad_key[:, key_lower:key_lower + key_width], key_weight[:, key_lower:key_lower + key_width], back_contract, preferred_element_type=jnp.float32)
        group_term = group_term + lax.dot_general(grad_value[:, key_lower:key_lower + key_width], value_weight[:, key_lower:key_lower + key_width], back_contract, preferred_element_type=jnp.float32)
        input_sum = input_sum + lax.optimization_barrier(group_term.astype(jnp.bfloat16)).astype(jnp.float32)
    return (attention, input_sum.astype(jnp.bfloat16), query_weight_grad, key_weight_grad, value_weight_grad)
```

```python
import functools
import math

import jax
import jax.numpy as jnp
from jax import lax
from jax.experimental import pallas as pl
from jax.experimental.pallas import tpu as pltpu
from jax.sharding import PartitionSpec as P

HEAD_DIM = 128
WINDOW = 1024
SCALAR = 168
HEADS = 16
KV_HEADS = 8
GROUP = HEADS // KV_HEADS
TILE = 256
LOW = -1e30
F32 = jnp.float32
BF16 = jnp.bfloat16
VMEM_LIMIT = 48 * 1024 * 1024


def passed_along(block, axis, distance):
    devices = range(lax.axis_size(axis))
    route = [(i - distance, i) for i in devices if i - distance in devices]
    return lax.ppermute(block, axis, route)


def rotated(block, axis, distance):
    size = lax.axis_size(axis)
    return lax.ppermute(block, axis, [(i, (i + distance) % size) for i in range(size)])


def rope_tables(positions):
    half_size = HEAD_DIM // 2
    indices = jnp.arange(half_size, dtype=F32)
    inverse = jnp.exp(indices * (-2.0 * math.log(10000.0) / HEAD_DIM))
    angles = positions.astype(F32)[:, None] * inverse[None, :]
    cosine, sine = jnp.cos(angles), jnp.sin(angles)
    return (
        jnp.concatenate([cosine, cosine], axis=1),
        jnp.concatenate([-sine, sine], axis=1),
    )


def head_map(u, cosine, sine, gain, factor):
    scale = lax.rsqrt(jnp.mean(u * u, axis=-1, keepdims=True) + 1e-06)
    normed = u * scale * gain
    turned = normed * cosine + pltpu.roll(normed, HEAD_DIM // 2, 1) * sine
    return turned * factor


def head_map_back(u, cosine, sine, gain, factor, cot):
    scale = lax.rsqrt(jnp.mean(u * u, axis=-1, keepdims=True) + 1e-06)
    cot = cot * factor
    inner = (cot * cosine + pltpu.roll(cot * sine, HEAD_DIM // 2, 1)) * gain
    mean = jnp.mean(inner * u, axis=-1, keepdims=True)
    return scale * inner - u * (scale * scale * scale * mean)


def key_kernel(key_ref, value_ref, cos_ref, sin_ref, gain_ref, pair_ref):
    pair_ref[0] = head_map(key_ref[...], cos_ref[...], sin_ref[...], gain_ref[...], 1.0).astype(BF16)
    pair_ref[1] = value_ref[...].astype(BF16)


def key_grad_kernel(reach, key_ref, cos_ref, sin_ref, gain_ref, own_ref, *rest):
    received, (key_out, value_out) = rest[:reach], rest[reach:]
    key_cot, value_cot = own_ref[0], own_ref[1]
    for ref in received:
        key_cot += ref[0].astype(F32)
        value_cot += ref[1].astype(F32)
    key_out[...] = head_map_back(
        key_ref[...], cos_ref[...], sin_ref[...], gain_ref[...], 1.0, key_cot
    ).astype(BF16)
    value_out[...] = value_cot.astype(BF16)


def dot_nt(a, b):
    return lax.dot_general(a, b, (((1,), (1,)), ((), ())), preferred_element_type=F32)


def dot_nn(a, b):
    return jnp.dot(a, b, preferred_element_type=F32)


def attention_kernel(
    rows, base_ref, query_ref, out_grad_ref, span_ref, cos_ref, sin_ref, gain_ref,
    attention_ref, query_grad_ref, own_ref, far_ref, total,
):
    chunks = WINDOW // TILE + 1
    factor = SCALAR ** (-0.5)
    base = base_ref[0]
    total[...] = jnp.zeros_like(total)
    key_turned = span_ref[0].T
    value_turned = span_ref[1].T
    row = lax.broadcasted_iota(jnp.int32, (TILE, TILE), 0)
    column = lax.broadcasted_iota(jnp.int32, (TILE, TILE), 1)
    for part in range(rows // TILE):
        at = slice(part * TILE, (part + 1) * TILE)
        keys = [slice((part + c) * TILE, (part + c + 1) * TILE) for c in range(chunks)]
        shift = [
            jnp.where(base - WINDOW + (part + c) * TILE >= 0, 0.0, LOW).astype(F32)
            for c in range(chunks)
        ]
        for head in range(GROUP):
            lanes = slice(head * HEAD_DIM, (head + 1) * HEAD_DIM)
            proj = query_ref[at, lanes]
            query = head_map(proj, cos_ref[at], sin_ref[at], gain_ref[...], factor).astype(BF16)
            out_grad = out_grad_ref[at, lanes]
            scores = [dot_nt(span_ref[0, key], query) for key in keys]
            scores[0] = jnp.where(row > column, scores[0], LOW)
            scores[-1] = jnp.where(row <= column, scores[-1], LOW)
            highest = jnp.full((1, TILE), LOW, F32)
            for s, b in zip(scores, shift):
                highest = jnp.maximum(highest, jnp.max(s, axis=0, keepdims=True) + b)
            weights = [jnp.exp(s - (highest - b)) for s, b in zip(scores, shift)]
            sums = jnp.sum(weights[0], axis=0, keepdims=True)
            for w in weights[1:]:
                sums += jnp.sum(w, axis=0, keepdims=True)
            inverse = 1.0 / sums
            weights = [w * inverse for w in weights]
            low = [w.astype(BF16) for w in weights]
            output = dot_nn(value_turned[:, keys[0]], low[0])
            for key, w in zip(keys[1:], low[1:]):
                output += dot_nn(value_turned[:, key], w)
            output = output.astype(BF16)
            attention_ref[at, lanes] = output.T
            delta = jnp.sum(
                out_grad.T.astype(F32) * output.astype(F32), axis=0, keepdims=True
            )
            query_cot = jnp.zeros((HEAD_DIM, TILE), F32)
            for key, w, wl in zip(keys, weights, low):
                products = dot_nt(span_ref[1, key], out_grad)
                moves = (w * (products - delta)).astype(BF16)
                query_cot += dot_nn(key_turned[:, key], moves)
                total[0, key] += dot_nn(moves, query)
                total[1, key] += dot_nn(wl, out_grad)
            query_grad_ref[at, lanes] = head_map_back(
                proj, cos_ref[at], sin_ref[at], gain_ref[...], factor, query_cot.T
            ).astype(BF16)
    far_ref[...] = total[:, :WINDOW].astype(BF16)
    own_ref[...] = total[:, WINDOW:]


def params():
    return pltpu.CompilerParams(vmem_limit_bytes=VMEM_LIMIT)


def whole(shape):
    return pl.BlockSpec(shape, lambda h: (0,) * len(shape))


def per_head(rows, width=HEAD_DIM):
    return pl.BlockSpec((rows, width), lambda h: (0, h))


def pair_head(rows):
    return pl.BlockSpec((2, rows, HEAD_DIM), lambda h: (0, 0, h))


def per_device(hidden, query_weight, key_weight, value_weight, query_gain, key_gain, out_grad):
    rows = out_grad.shape[0]
    share, depth = hidden.shape
    peers = lax.axis_size("heads")
    me = lax.axis_index("heads")
    reach = WINDOW // rows
    base = lax.axis_index("ctx") * rows
    query_width, key_width = query_weight.shape[1], key_weight.shape[1]
    kv_heads = key_width // HEAD_DIM

    pieces = 3
    step = depth // pieces
    gathered, query_proj, key_proj, value_proj = [], None, None, None
    for piece in range(pieces):
        span = slice(piece * step, (piece + 1) * step)
        mine = hidden[:, span]
        block = jnp.zeros((rows, step), BF16)
        block = lax.dynamic_update_slice(block, mine, (me * share, 0))
        for distance in range(1, peers):
            other = rotated(mine, "heads", distance)
            block = lax.dynamic_update_slice(
                block, other, (lax.rem(me + peers - distance, peers) * share, 0)
            )
        gathered.append(block)
        q = dot_nn(block, query_weight[span])
        k = dot_nn(block, key_weight[span])
        v = dot_nn(block, value_weight[span])
        query_proj = q if query_proj is None else query_proj + q
        key_proj = k if key_proj is None else key_proj + k
        value_proj = v if value_proj is None else value_proj + v

    cosine, sine = rope_tables(base + jnp.arange(rows, dtype=jnp.int32))
    query_gain, key_gain = query_gain[None, :], key_gain[None, :]
    table = whole((rows, HEAD_DIM))
    gain = whole((1, HEAD_DIM))
    pair = pl.pallas_call(
        key_kernel,
        grid=(kv_heads,),
        in_specs=[per_head(rows), per_head(rows), table, table, gain],
        out_specs=pair_head(rows),
        out_shape=jax.ShapeDtypeStruct((2, rows, key_width), BF16),
        compiler_params=params(),
    )(key_proj, value_proj, cosine, sine, key_gain)
    received = [passed_along(pair, "ctx", distance) for distance in range(1, reach + 1)]
    span = jnp.concatenate(received[::-1] + [pair], axis=1)

    attention, grad_query, own, far = pl.pallas_call(
        functools.partial(attention_kernel, rows),
        grid=(kv_heads,),
        in_specs=[
            pl.BlockSpec(memory_space=pltpu.SMEM),
            per_head(rows, GROUP * HEAD_DIM),
            per_head(rows, GROUP * HEAD_DIM),
            pair_head(rows + WINDOW),
            table,
            table,
            gain,
        ],
        out_specs=[
            per_head(rows, GROUP * HEAD_DIM),
            per_head(rows, GROUP * HEAD_DIM),
            pair_head(rows),
            pair_head(WINDOW),
        ],
        out_shape=[
            jax.ShapeDtypeStruct((rows, query_width), BF16),
            jax.ShapeDtypeStruct((rows, query_width), BF16),
            jax.ShapeDtypeStruct((2, rows, key_width), F32),
            jax.ShapeDtypeStruct((2, WINDOW, key_width), BF16),
        ],
        scratch_shapes=[pltpu.VMEM((2, rows + WINDOW, HEAD_DIM), F32)],
        compiler_params=params(),
    )(base[None], query_proj, out_grad, span, cosine, sine, query_gain)

    tokens = jnp.concatenate(gathered, axis=1)
    grad_scale = float(lax.axis_size("ctx") * rows) ** (-0.5)

    def weight_grad(columns):
        partial = (
            lax.dot_general(
                tokens, columns, (((0,), (0,)), ((), ())), preferred_element_type=F32
            )
            * grad_scale
        ).astype(BF16)
        return lax.psum_scatter(partial, "ctx", scatter_dimension=0, tiled=True).astype(F32)

    query_weight_grad = weight_grad(grad_query)
    backs = [
        passed_along(far[:, (reach - distance) * rows : (reach - distance + 1) * rows], "ctx", -distance)
        for distance in range(1, reach + 1)
    ]
    grad_key, grad_value = pl.pallas_call(
        functools.partial(key_grad_kernel, reach),
        grid=(kv_heads,),
        in_specs=[per_head(rows), table, table, gain] + [pair_head(rows)] * (1 + reach),
        out_specs=[per_head(rows), per_head(rows)],
        out_shape=[jax.ShapeDtypeStruct((rows, key_width), BF16)] * 2,
        compiler_params=params(),
    )(key_proj, cosine, sine, key_gain, own, *backs)

    def input_term(owner):
        def cut(array):
            return lax.dynamic_slice_in_dim(array, owner * share, share, 0)

        return (
            dot_nt(cut(grad_query), query_weight)
            + dot_nt(cut(grad_key), key_weight)
            + dot_nt(cut(grad_value), value_weight)
        ).astype(BF16)

    arrived = [
        rotated(input_term(lax.rem(me + distance, peers)), "heads", distance)
        for distance in range(1, peers)
    ]
    pair_weight_grad = weight_grad(jnp.concatenate([grad_key, grad_value], axis=1))
    input_sum = input_term(me).astype(F32)
    for term in arrived:
        input_sum += term.astype(F32)
    return (
        attention,
        input_sum.astype(BF16),
        query_weight_grad,
        pair_weight_grad[:, :key_width],
        pair_weight_grad[:, key_width:],
    )


def solution(mesh):
    return jax.shard_map(
        per_device,
        mesh=mesh,
        in_specs=(
            P(("ctx", "heads"), None),
            P(None, "heads"),
            P(None, "heads"),
            P(None, "heads"),
            P(),
            P(),
            P("ctx", "heads"),
        ),
        out_specs=(
            P("ctx", "heads"),
            P(("ctx", "heads"), None),
            P("ctx", "heads"),
            P("ctx", "heads"),
            P("ctx", "heads"),
        ),
        check_vma=False,
    )
```

```python
import functools
import math

import jax
import jax.numpy as jnp
from jax import lax
from jax.experimental import pallas as pl
from jax.experimental.pallas import tpu as pltpu
from jax.sharding import PartitionSpec as P

HEAD_DIM = 128
WINDOW = 1024
SCALAR = 168
HEADS = 16
KV_HEADS = 8
GROUP = HEADS // KV_HEADS
TILE = 256
LOW = -1e30
F32 = jnp.float32
BF16 = jnp.bfloat16
VMEM_LIMIT = 48 * 1024 * 1024


def passed_along(block, axis, distance):
    devices = range(lax.axis_size(axis))
    route = [(i - distance, i) for i in devices if i - distance in devices]
    return lax.ppermute(block, axis, route)


def rotated(block, axis, distance):
    size = lax.axis_size(axis)
    return lax.ppermute(block, axis, [(i, (i + distance) % size) for i in range(size)])


def rope_tables(positions):
    half_size = HEAD_DIM // 2
    indices = jnp.arange(half_size, dtype=F32)
    inverse = jnp.exp(indices * (-2.0 * math.log(10000.0) / HEAD_DIM))
    angles = positions.astype(F32)[:, None] * inverse[None, :]
    cosine, sine = jnp.cos(angles), jnp.sin(angles)
    return (
        jnp.concatenate([cosine, cosine], axis=1),
        jnp.concatenate([-sine, sine], axis=1),
    )


def head_map(u, cosine, sine, gain, factor):
    scale = lax.rsqrt(jnp.mean(u * u, axis=-1, keepdims=True) + 1e-06)
    normed = u * scale * gain
    turned = normed * cosine + pltpu.roll(normed, HEAD_DIM // 2, 1) * sine
    return turned * factor


def head_map_back(u, cosine, sine, gain, factor, cot):
    scale = lax.rsqrt(jnp.mean(u * u, axis=-1, keepdims=True) + 1e-06)
    cot = cot * factor
    inner = (cot * cosine + pltpu.roll(cot * sine, HEAD_DIM // 2, 1)) * gain
    mean = jnp.mean(inner * u, axis=-1, keepdims=True)
    return scale * inner - u * (scale * scale * scale * mean)


def key_kernel(key_ref, value_ref, cos_ref, sin_ref, gain_ref, pair_ref):
    pair_ref[0] = head_map(key_ref[...], cos_ref[...], sin_ref[...], gain_ref[...], 1.0).astype(BF16)
    pair_ref[1] = value_ref[...].astype(BF16)


def key_grad_kernel(reach, key_ref, cos_ref, sin_ref, gain_ref, own_ref, *rest):
    received, (key_out, value_out) = rest[:reach], rest[reach:]
    key_cot, value_cot = own_ref[0], own_ref[1]
    for ref in received:
        key_cot += ref[0].astype(F32)
        value_cot += ref[1].astype(F32)
    key_out[...] = head_map_back(
        key_ref[...], cos_ref[...], sin_ref[...], gain_ref[...], 1.0, key_cot
    ).astype(BF16)
    value_out[...] = value_cot.astype(BF16)


def dot_nt(a, b):
    return lax.dot_general(a, b, (((1,), (1,)), ((), ())), preferred_element_type=F32)


def dot_nn(a, b):
    return jnp.dot(a, b, preferred_element_type=F32)


def attention_kernel(
    rows, base_ref, query_ref, out_grad_ref, span_ref, cos_ref, sin_ref, gain_ref,
    attention_ref, query_grad_ref, own_ref, far_ref, total,
):
    chunks = WINDOW // TILE + 1
    factor = SCALAR ** (-0.5)
    base = base_ref[0]
    total[...] = jnp.zeros_like(total)
    key_turned = span_ref[0].T
    value_turned = span_ref[1].T
    row = lax.broadcasted_iota(jnp.int32, (TILE, TILE), 0)
    column = lax.broadcasted_iota(jnp.int32, (TILE, TILE), 1)
    for part in range(rows // TILE):
        at = slice(part * TILE, (part + 1) * TILE)
        keys = [slice((part + c) * TILE, (part + c + 1) * TILE) for c in range(chunks)]
        shift = [
            jnp.where(base - WINDOW + (part + c) * TILE >= 0, 0.0, LOW).astype(F32)
            for c in range(chunks)
        ]
        for head in range(GROUP):
            lanes = slice(head * HEAD_DIM, (head + 1) * HEAD_DIM)
            proj = query_ref[at, lanes]
            query = head_map(proj, cos_ref[at], sin_ref[at], gain_ref[...], factor).astype(BF16)
            out_grad = out_grad_ref[at, lanes]
            scores = [dot_nt(span_ref[0, key], query) for key in keys]
            scores[0] = jnp.where(row > column, scores[0], LOW)
            scores[-1] = jnp.where(row <= column, scores[-1], LOW)
            highest = jnp.full((1, TILE), LOW, F32)
            for s, b in zip(scores, shift):
                highest = jnp.maximum(highest, jnp.max(s, axis=0, keepdims=True) + b)
            weights = [jnp.exp(s - (highest - b)) for s, b in zip(scores, shift)]
            sums = jnp.sum(weights[0], axis=0, keepdims=True)
            for w in weights[1:]:
                sums += jnp.sum(w, axis=0, keepdims=True)
            inverse = 1.0 / sums
            weights = [w * inverse for w in weights]
            low = [w.astype(BF16) for w in weights]
            output = dot_nn(value_turned[:, keys[0]], low[0])
            for key, w in zip(keys[1:], low[1:]):
                output += dot_nn(value_turned[:, key], w)
            output = output.astype(BF16)
            attention_ref[at, lanes] = output.T
            delta = jnp.sum(
                out_grad.T.astype(F32) * output.astype(F32), axis=0, keepdims=True
            )
            query_cot = jnp.zeros((HEAD_DIM, TILE), F32)
            for key, w, wl in zip(keys, weights, low):
                products = dot_nt(span_ref[1, key], out_grad)
                moves = (w * (products - delta)).astype(BF16)
                query_cot += dot_nn(key_turned[:, key], moves)
                total[0, key] += dot_nn(moves, query)
                total[1, key] += dot_nn(wl, out_grad)
            query_grad_ref[at, lanes] = head_map_back(
                proj, cos_ref[at], sin_ref[at], gain_ref[...], factor, query_cot.T
            ).astype(BF16)
    far_ref[...] = total[:, :WINDOW].astype(BF16)
    own_ref[...] = total[:, WINDOW:]


def params():
    return pltpu.CompilerParams(vmem_limit_bytes=VMEM_LIMIT)


def whole(shape):
    return pl.BlockSpec(shape, lambda h: (0,) * len(shape))


def per_head(rows, width=HEAD_DIM):
    return pl.BlockSpec((rows, width), lambda h: (0, h))


def pair_head(rows):
    return pl.BlockSpec((2, rows, HEAD_DIM), lambda h: (0, 0, h))


def per_device(hidden, query_weight, key_weight, value_weight, query_gain, key_gain, out_grad):
    rows = out_grad.shape[0]
    share, depth = hidden.shape
    peers = lax.axis_size("heads")
    me = lax.axis_index("heads")
    reach = WINDOW // rows
    base = lax.axis_index("ctx") * rows
    query_width, key_width = query_weight.shape[1], key_weight.shape[1]
    kv_heads = key_width // HEAD_DIM

    pieces = 3
    step = depth // pieces
    gathered, query_proj, key_proj, value_proj = [], None, None, None
    for piece in range(pieces):
        span = slice(piece * step, (piece + 1) * step)
        mine = hidden[:, span]
        block = jnp.zeros((rows, step), BF16)
        block = lax.dynamic_update_slice(block, mine, (me * share, 0))
        for distance in range(1, peers):
            other = rotated(mine, "heads", distance)
            block = lax.dynamic_update_slice(
                block, other, (lax.rem(me + peers - distance, peers) * share, 0)
            )
        gathered.append(block)
        q = dot_nn(block, query_weight[span])
        k = dot_nn(block, key_weight[span])
        v = dot_nn(block, value_weight[span])
        query_proj = q if query_proj is None else query_proj + q
        key_proj = k if key_proj is None else key_proj + k
        value_proj = v if value_proj is None else value_proj + v

    cosine, sine = rope_tables(base + jnp.arange(rows, dtype=jnp.int32))
    query_gain, key_gain = query_gain[None, :], key_gain[None, :]
    table = whole((rows, HEAD_DIM))
    gain = whole((1, HEAD_DIM))
    pair = pl.pallas_call(
        key_kernel,
        grid=(kv_heads,),
        in_specs=[per_head(rows), per_head(rows), table, table, gain],
        out_specs=pair_head(rows),
        out_shape=jax.ShapeDtypeStruct((2, rows, key_width), BF16),
        compiler_params=params(),
    )(key_proj, value_proj, cosine, sine, key_gain)
    received = [passed_along(pair, "ctx", distance) for distance in range(1, reach + 1)]
    span = jnp.concatenate(received[::-1] + [pair], axis=1)

    attention, grad_query, own, far = pl.pallas_call(
        functools.partial(attention_kernel, rows),
        grid=(kv_heads,),
        in_specs=[
            pl.BlockSpec(memory_space=pltpu.SMEM),
            per_head(rows, GROUP * HEAD_DIM),
            per_head(rows, GROUP * HEAD_DIM),
            pair_head(rows + WINDOW),
            table,
            table,
            gain,
        ],
        out_specs=[
            per_head(rows, GROUP * HEAD_DIM),
            per_head(rows, GROUP * HEAD_DIM),
            pair_head(rows),
            pair_head(WINDOW),
        ],
        out_shape=[
            jax.ShapeDtypeStruct((rows, query_width), BF16),
            jax.ShapeDtypeStruct((rows, query_width), BF16),
            jax.ShapeDtypeStruct((2, rows, key_width), F32),
            jax.ShapeDtypeStruct((2, WINDOW, key_width), BF16),
        ],
        scratch_shapes=[pltpu.VMEM((2, rows + WINDOW, HEAD_DIM), F32)],
        compiler_params=params(),
    )(base[None], query_proj, out_grad, span, cosine, sine, query_gain)

    tokens = jnp.concatenate(gathered, axis=1)
    grad_scale = float(lax.axis_size("ctx") * rows) ** (-0.5)

    def weight_grad(columns):
        partial = (
            lax.dot_general(
                tokens, columns, (((0,), (0,)), ((), ())), preferred_element_type=F32
            )
            * grad_scale
        ).astype(BF16)
        return lax.psum_scatter(partial, "ctx", scatter_dimension=0, tiled=True).astype(F32)

    backs = [
        passed_along(far[:, (reach - distance) * rows : (reach - distance + 1) * rows], "ctx", -distance)
        for distance in range(1, reach + 1)
    ]
    grad_key, grad_value = pl.pallas_call(
        functools.partial(key_grad_kernel, reach),
        grid=(kv_heads,),
        in_specs=[per_head(rows), table, table, gain] + [pair_head(rows)] * (1 + reach),
        out_specs=[per_head(rows), per_head(rows)],
        out_shape=[jax.ShapeDtypeStruct((rows, key_width), BF16)] * 2,
        compiler_params=params(),
    )(key_proj, cosine, sine, key_gain, own, *backs)

    def input_term(owner):
        def cut(array):
            return lax.dynamic_slice_in_dim(array, owner * share, share, 0)

        return (
            dot_nt(cut(grad_query), query_weight)
            + dot_nt(cut(grad_key), key_weight)
            + dot_nt(cut(grad_value), value_weight)
        ).astype(BF16)

    arrived = [
        rotated(input_term(lax.rem(me + distance, peers)), "heads", distance)
        for distance in range(1, peers)
    ]
    summed = weight_grad(jnp.concatenate([grad_query, grad_key, grad_value], axis=1))
    input_sum = input_term(me).astype(F32)
    for term in arrived:
        input_sum += term.astype(F32)
    return (
        attention,
        input_sum.astype(BF16),
        summed[:, :query_width],
        summed[:, query_width : query_width + key_width],
        summed[:, query_width + key_width :],
    )


def solution(mesh):
    return jax.shard_map(
        per_device,
        mesh=mesh,
        in_specs=(
            P(("ctx", "heads"), None),
            P(None, "heads"),
            P(None, "heads"),
            P(None, "heads"),
            P(),
            P(),
            P("ctx", "heads"),
        ),
        out_specs=(
            P("ctx", "heads"),
            P(("ctx", "heads"), None),
            P("ctx", "heads"),
            P("ctx", "heads"),
            P("ctx", "heads"),
        ),
        check_vma=False,
    )
```
